32 devices in a mesh: grp: 2 (over y), pair: 4 (over z), dir: 2 (over x), pol: 2 (over core).
Axes of the slice: x: 2, y: 2, z: 4, core: 2. Of those that a mesh axis runs over, the one named last changes fastest.
Arguments:
- blocks: int32 [40, 2], P(('grp', 'pair')), parts along dimension 0, may hold values from 0 to 3, as said below
- counts: int32 [8], P(('grp', 'pair')), parts along dimension 0, may hold values from 1 to 5, as said below
- gains: float32 [16, 2, 8, 512], P(('grp', 'dir'), None, None, 'pair'), parts along dimension 0, may hold values from -1.5 to 1.5
- coherency: bfloat16 [40, 2, 8, 2, 8, 16384], P(('grp', 'pair'), 'pol', 'dir'), parts along dimension 0, may hold values from -6 to 6
- observed: bfloat16 [40, 2, 2, 8, 16384], P(('grp', 'pair'), 'pol'), parts along dimension 0, may hold values from -6 to 6
Outputs:
- residual: bfloat16 [40, 2, 2, 8, 16384], P(('grp', 'pair'), 'pol'), parts along dimension 0
- gradient: float32 [16, 2, 8, 512], P(('grp', 'dir'), None, None, ('pair', 'pol')), parts along dimension 0
The draws below stay inside these ranges and needn't reach their ends.
There are 2 independent parts, one for each index of `grp`. The reference program is written for one: setup_inputs(seed, part) draws one part's arguments, and reference() takes and returns one part's arrays. A program takes and returns all parts, laid end to end along the dimension named above; each array names one. Nothing has to cross between parts.
Inputs may be any that keep to these rules, and one draw needn't show every extreme that they name: `blocks`: over the used slots every block pair (a, b) with a <= b appears exactly once, a <= b; an unused slot repeats the last used pair of its pair index. `counts`: they sum to 10; some pair index uses all 5 slots.
All inputs are finite; a program needn't handle non-finite values.
Results may differ from the reference program's by a relative error of at most 0.007.
Values may be sent and summed in bfloat16 or wider, within the bound.
A program may use at most 384 MiB of HBM per device.

```python
import jax
import jax.numpy as jnp
import numpy as np
from jax import lax

STATIONS = 512
DIRS = 8
CHANS = 2
DUMPS = 2
DIRS_DEV = 4
BLK = 128
BASE = 16384
BLK_PAIRS = 10
MAXB = 5
SLOTS = 20
N_PAIR = 4
N_DIR = 2


def slot_layout(key):
    key_order, key_moved, key_shuffle = jax.random.split(key, 3)
    order = jax.random.permutation(key_order, N_PAIR)
    index = jnp.arange(N_PAIR, dtype=jnp.int32)
    extra = BLK_PAIRS - N_PAIR * (N_PAIR // 2)
    base = N_PAIR // 2 + (index < extra).astype(jnp.int32)
    rank = jnp.zeros((N_PAIR,), jnp.int32).at[order].set(index)
    busiest = order[0]
    excess = MAXB - base[busiest]
    tallies = base - ((rank >= 1) & (rank <= excess)).astype(jnp.int32)
    tallies = tallies.at[busiest].set(MAXB)
    npairs = (N_PAIR - 1) // 2
    givers = order[1:1 + 2 * npairs:2]
    takers = order[2:2 + 2 * npairs:2]
    limit = jnp.minimum(MAXB - tallies[takers], tallies[givers] - 1)
    moved = jax.random.randint(key_moved, (npairs,), 0, limit + 1).astype(jnp.int32)
    tallies = tallies.at[takers].add(moved).at[givers].add(-moved)
    upper_rows, upper_cols = np.triu_indices(N_PAIR)
    upper_rows = jnp.asarray(upper_rows, jnp.int32)
    upper_cols = jnp.asarray(upper_cols, jnp.int32)
    shuffle = jax.random.permutation(key_shuffle, BLK_PAIRS)
    starts = jnp.cumsum(tallies) - tallies
    slot_index = jnp.arange(SLOTS, dtype=jnp.int32)
    device = slot_index // MAXB
    position = jnp.minimum(slot_index % MAXB, tallies[device] - 1)
    picked = shuffle[starts[device] + position]
    pair_list = jnp.stack([upper_rows[picked], upper_cols[picked]], axis=1).astype(jnp.int32)
    return (tallies.astype(jnp.int32), pair_list)


def draw_blocks(key, part):
    layout = slot_layout(key)
    return layout[1]


def draw_counts(key, part):
    layout = slot_layout(key)
    return layout[0]


def level_of(key, shape, cuts, least, top_value):
    level = 1.0
    for axis_at, shards_of in cuts:
        draws = jax.random.uniform(jax.random.fold_in(jax.random.fold_in(key, 6), axis_at), (shards_of,), jnp.float32, least / len(cuts), top_value / len(cuts))
        level = level * jnp.repeat(jnp.exp(draws), shape[axis_at] // shards_of).reshape((-1,) + (1,) * (len(shape) - 1 - axis_at))
    return level


def scatter_about(rng, shape, width, bound, pieces=(), kind=jnp.bfloat16):
    entries = width * jax.random.normal(rng, shape, jnp.float32)
    if pieces:
        entries = entries * level_of(rng, shape, pieces, -0.22, 0.18)
    return jnp.clip(entries, -bound, bound).astype(kind)


def setup_inputs(seed: int = 0, part: int = 0) -> dict:
    streams_of = jax.random.split(jax.random.key(seed), 6)
    own_keys = jax.random.split(jax.random.fold_in(streams_of[5], part), 6)
    blocks = draw_blocks(jax.random.fold_in(jax.random.fold_in(streams_of[5], part), 71), part)
    counts = draw_counts(jax.random.fold_in(jax.random.fold_in(streams_of[5], part), 71), part)
    gains = scatter_about(own_keys[2], (DIRS, CHANS, 8, STATIONS), 0.25, 1.5, ((0, 2), (3, 4)), jnp.float32)
    coherency = scatter_about(own_keys[3], (SLOTS, DUMPS, DIRS, CHANS, 8, BASE), 1.0, 6.0, ((0, 4), (1, 2), (2, 2)))
    observed = scatter_about(own_keys[4], (SLOTS, DUMPS, CHANS, 8, BASE), 1.0, 6.0, ((0, 4), (1, 2)))
    return dict(blocks=blocks, counts=counts, gains=gains, coherency=coherency, observed=observed)


def split_parts(matrix, axis):
    return [lax.index_in_dim(matrix, c, axis, keepdims=False) for c in range(8)]


def product(left, right):
    result = [None] * 8
    for row_index in range(2):
        for col_index in range(2):
            real_sum = 0.0
            imag_sum = 0.0
            for mid_index in range(2):
                left_re = left[2 * row_index + mid_index]
                left_im = left[4 + 2 * row_index + mid_index]
                right_re = right[2 * mid_index + col_index]
                right_im = right[4 + 2 * mid_index + col_index]
                real_sum = real_sum + left_re * right_re - left_im * right_im
                imag_sum = imag_sum + left_re * right_im + left_im * right_re
            result[2 * row_index + col_index] = real_sum
            result[4 + 2 * row_index + col_index] = imag_sum
    return result


def adjoint(matrix):
    return [matrix[0], matrix[2], matrix[1], matrix[3], -matrix[4], -matrix[6], -matrix[5], -matrix[7]]


def direction_gains(one_dir, first, second, nblocks, blk):
    table = one_dir.reshape(one_dir.shape[0], 8, nblocks, blk)
    gain_a = jnp.moveaxis(jnp.take(table, first, axis=2), 2, 0)
    gain_b = jnp.moveaxis(jnp.take(table, second, axis=2), 2, 0)
    left_g = jnp.repeat(gain_a, blk, axis=3)[:, None]
    right_g = jnp.tile(gain_b, (1, 1, 1, blk))[:, None]
    return split_parts(left_g, 3), split_parts(right_g, 3)


def baseline_mask(first, second, used, blk):
    pair_index = jnp.arange(blk * blk)
    upper = (pair_index // blk) < (pair_index % blk)
    keep = used[:, None] & ((first < second)[:, None] | upper[None, :])
    return keep.astype(jnp.float32)[:, None, None, None, :]


def reference(blocks, counts, gains, coherency, observed):
    slot_index = jnp.arange(SLOTS)
    used = (slot_index % MAXB) < counts[slot_index // MAXB]
    first = blocks[:, 0]
    second = blocks[:, 1]
    mask = baseline_mask(first, second, used, BLK)
    predicted = jnp.zeros(observed.shape, jnp.float32)
    for group in range(N_DIR):
        partial_sum = jnp.zeros(observed.shape, jnp.float32)
        for local in range(DIRS_DEV):
            direction = group * DIRS_DEV + local
            left_g, right_g = direction_gains(gains[direction], first, second, N_PAIR, BLK)
            model_c = split_parts(coherency[:, :, direction].astype(jnp.float32), 3)
            partial_sum = partial_sum + jnp.stack(product(product(left_g, model_c), adjoint(right_g)), axis=3)
        rounded = lax.optimization_barrier(partial_sum.astype(jnp.bfloat16))
        predicted = predicted + rounded.astype(jnp.float32)
    residual = (mask * (observed.astype(jnp.float32) - predicted)).astype(jnp.bfloat16)
    resid_parts = split_parts(residual.astype(jnp.float32), 3)
    onehot_first = (first[:, None] == jnp.arange(N_PAIR)[None, :]).astype(jnp.float32)
    onehot_second = (second[:, None] == jnp.arange(N_PAIR)[None, :]).astype(jnp.float32)
    grads = []
    for direction in range(DIRS):
        left_g, right_g = direction_gains(gains[direction], first, second, N_PAIR, BLK)
        model_c = split_parts(coherency[:, :, direction].astype(jnp.float32), 3)
        toward_first = jnp.stack(product(resid_parts, product(right_g, adjoint(model_c))), axis=3)
        toward_second = jnp.stack(product(adjoint(resid_parts), product(left_g, model_c)), axis=3)
        toward_first = jnp.sum(toward_first, axis=1).reshape(SLOTS, CHANS, 8, BLK, BLK).sum(axis=4)
        toward_second = jnp.sum(toward_second, axis=1).reshape(SLOTS, CHANS, 8, BLK, BLK).sum(axis=3)
        grad_dir = jnp.einsum("scxb,sn->cxnb", toward_first, onehot_first, precision=lax.Precision.HIGHEST)
        grad_dir = grad_dir + jnp.einsum("scxb,sn->cxnb", toward_second, onehot_second, precision=lax.Precision.HIGHEST)
        grads.append(grad_dir.reshape(CHANS, 8, STATIONS))
    return residual, jnp.stack(grads, axis=0)
```

```python
import functools

import jax
import jax.numpy as jnp
from jax import lax
from jax.experimental import pallas as pl
from jax.experimental.pallas import tpu as pltpu
from jax.sharding import PartitionSpec as P

LANES = 128
CHUNK = 64


def split_parts(matrix, axis):
    return [lax.index_in_dim(matrix, c, axis, keepdims=False) for c in range(8)]


def product(left, right):
    result = [None] * 8
    for i in range(2):
        for j in range(2):
            re = im = None
            for m in range(2):
                lr, li = left[2 * i + m], left[4 + 2 * i + m]
                rr, ri = right[2 * m + j], right[4 + 2 * m + j]
                re_term = lr * rr - li * ri
                im_term = lr * ri + li * rr
                re = re_term if re is None else re + re_term
                im = im_term if im is None else im + im_term
            result[2 * i + j] = re
            result[4 + 2 * i + j] = im
    return result


def product_adj_right(left, right):
    result = [None] * 8
    for i in range(2):
        for j in range(2):
            re = im = None
            for m in range(2):
                lr, li = left[2 * i + m], left[4 + 2 * i + m]
                rr, ri = right[2 * j + m], right[4 + 2 * j + m]
                re_term = lr * rr + li * ri
                im_term = li * rr - lr * ri
                re = re_term if re is None else re + re_term
                im = im_term if im is None else im + im_term
            result[2 * i + j] = re
            result[4 + 2 * i + j] = im
    return result


def product_adj_left(left, right):
    result = [None] * 8
    for i in range(2):
        for j in range(2):
            re = im = None
            for m in range(2):
                lr, li = left[2 * m + i], left[4 + 2 * m + i]
                rr, ri = right[2 * m + j], right[4 + 2 * m + j]
                re_term = lr * rr + li * ri
                im_term = lr * ri - li * rr
                re = re_term if re is None else re + re_term
                im = im_term if im is None else im + im_term
            result[2 * i + j] = re
            result[4 + 2 * i + j] = im
    return result


def adjoint(m):
    return [m[0], m[2], m[1], m[3], -m[4], -m[6], -m[5], -m[7]]


def widen(src, dst, dirs):
    for k in range(dirs):
        for p in range(CHUNK):
            dst[k, p * 8 : p * 8 + 8, :] = src[0, 0, k, 0, :, p * LANES : (p + 1) * LANES].astype(
                jnp.float32
            )


def parts_at(ref, k, row):
    return [ref[k, pl.ds(row + c, 8, stride=8), :] for c in range(8)]


def forward_kernel(dirs, blocks, left_ref, right_ref, coh_ref, out_ref, wide):
    widen(coh_ref, wide, dirs)

    @pl.loop(0, CHUNK // 16)
    def _(g):
        halves = []
        for h in range(2):
            p0 = pl.multiple_of(g * 16 + h * 8, 8)
            rows = left_ref[0, 0, pl.ds(p0, 8), :]
            total = None
            for k in range(dirs):
                model = parts_at(wide, k, pl.multiple_of(p0 * 8, 64))
                jq = [right_ref[0, 0, k * 8 + c : k * 8 + c + 1, :] for c in range(8)]
                jp = [rows[:, k * 8 + c : k * 8 + c + 1] for c in range(8)]
                term = product(jp, product_adj_right(model, jq))
                total = term if total is None else [x + y for x, y in zip(total, term)]
            halves.append(total)
        for c in range(8):
            both = jnp.concatenate([halves[0][c], halves[1][c]], axis=0)
            out_ref[0, c, pl.ds(pl.multiple_of(g * 16, 16), 16), :] = both.astype(jnp.bfloat16)


def backward_kernel(
    dirs,
    slot,
    blocks,
    counts,
    left_ref,
    right_ref,
    own_ref,
    other_ref,
    obs_ref,
    coh_ref,
    res_ref,
    first_ref,
    second_ref,
    wide,
    wide_obs,
    res,
    acc,
):
    chunk = pl.program_id(1)
    widen(coh_ref, wide, dirs)
    for p in range(CHUNK):
        wide_obs[0, p * 8 : p * 8 + 8, :] = obs_ref[0, 0, 0, :, p * LANES : (p + 1) * LANES].astype(
            jnp.float32
        )
    used = slot < counts[0]
    off_diag = blocks[slot, 0] < blocks[slot, 1]

    @pl.loop(0, CHUNK // 16)
    def _(g):
        r0 = pl.multiple_of(g * 16, 16)
        station = chunk * CHUNK + r0 + lax.broadcasted_iota(jnp.int32, (16, LANES), 0)
        partner = lax.broadcasted_iota(jnp.int32, (16, LANES), 1)
        upper = (jnp.where(off_diag, -1, station) < partner) & (jnp.where(used, partner, -1) >= 0)
        for c in range(8):
            predicted = own_ref[0, c, pl.ds(r0, 16), :].astype(jnp.float32) + other_ref[
                0, c, pl.ds(r0, 16), :
            ].astype(jnp.float32)
            seen = jnp.concatenate(
                [wide_obs[0, pl.ds((r0 + h * 8) * 8 + c, 8, stride=8), :] for h in range(2)], axis=0
            )
            left_over = jnp.where(upper, seen - predicted, 0.0).astype(jnp.bfloat16).astype(jnp.float32)
            res[c, pl.ds(r0, 16), :] = left_over
            for h in range(2):
                wide_obs[0, pl.ds((r0 + h * 8) * 8 + c, 8, stride=8), :] = left_over[h * 8 : h * 8 + 8]

    for p in range(CHUNK):
        res_ref[0, 0, 0, :, p * LANES : (p + 1) * LANES] = wide_obs[0, p * 8 : p * 8 + 8, :].astype(
            jnp.bfloat16
        )

    @pl.when(chunk == 0)
    def _():
        acc[...] = jnp.zeros_like(acc)

    for k in range(dirs):

        def step(g, sums, k=k):
            p0 = pl.multiple_of(g * 8, 8)
            model = parts_at(wide, k, pl.multiple_of(p0 * 8, 64))
            rest = [res[c, pl.ds(p0, 8), :] for c in range(8)]
            jq = [right_ref[0, 0, k * 8 + c : k * 8 + c + 1, :] for c in range(8)]
            rows = left_ref[0, 0, pl.ds(p0, 8), :]
            jp = [rows[:, k * 8 + c : k * 8 + c + 1] for c in range(8)]
            toward_first = product_adj_right(rest, product_adj_right(model, jq))
            for c in range(8):
                first_ref[0, pl.ds(p0, 8), k * 8 + c : k * 8 + c + 1] = jnp.sum(
                    toward_first[c], axis=1, keepdims=True
                )
            toward_second = product_adj_left(rest, product(jp, model))
            return tuple(x + y for x, y in zip(sums, toward_second))

        zero = jnp.zeros((8, LANES), jnp.float32)
        sums = lax.fori_loop(0, CHUNK // 8, step, (zero,) * 8)
        for c in range(8):
            acc[k * 8 + c] += sums[c]

    @pl.when(chunk == pl.num_programs(1) - 1)
    def _():
        second_ref[0] = jnp.sum(acc[...], axis=1)


def fast_body(blocks, counts, gains, coherency, observed):
    nblocks = lax.axis_size("pair")
    dirs, chans, _, blk = gains.shape
    maxb = blocks.shape[0]
    base = coherency.shape[-1]
    chunks = blk // CHUNK
    width = CHUNK * LANES
    comps = dirs * 8
    whole = lax.all_gather(gains, "pair", axis=0)
    right = jnp.transpose(whole, (0, 2, 1, 3, 4)).reshape(nblocks, chans, comps, blk)
    left = jnp.transpose(right, (0, 1, 3, 2))
    kind = pltpu.CompilerParams(
        dimension_semantics=("arbitrary", "arbitrary"), vmem_limit_bytes=40 * 2**20
    )
    ops = 64 * dirs * chans * base

    def forward(slot):
        return pl.pallas_call(
            functools.partial(forward_kernel, dirs),
            grid_spec=pltpu.PrefetchScalarGridSpec(
                num_scalar_prefetch=1,
                grid=(chans, chunks),
                in_specs=[
                    pl.BlockSpec((1, 1, CHUNK, comps), lambda f, i, b: (b[slot, 0], f, i, 0)),
                    pl.BlockSpec((1, 1, comps, blk), lambda f, i, b: (b[slot, 1], f, 0, 0)),
                    pl.BlockSpec((1, 1, dirs, 1, 8, width), lambda f, i, b: (slot, 0, 0, f, 0, i)),
                ],
                out_specs=pl.BlockSpec((1, 8, CHUNK, LANES), lambda f, i, b: (f, 0, i, 0)),
                scratch_shapes=[pltpu.VMEM((dirs, CHUNK * 8, LANES), jnp.float32)],
            ),
            out_shape=jax.ShapeDtypeStruct((chans, 8, blk, blk), jnp.bfloat16),
            compiler_params=kind,
            cost_estimate=pl.CostEstimate(
                flops=4 * ops, bytes_accessed=dirs * chans * 8 * base * 2, transcendentals=0
            ),
            name="forward",
        )(blocks, left, right, coherency)

    def backward(slot, own, other):
        return pl.pallas_call(
            functools.partial(backward_kernel, dirs, slot),
            grid_spec=pltpu.PrefetchScalarGridSpec(
                num_scalar_prefetch=2,
                grid=(chans, chunks),
                in_specs=[
                    pl.BlockSpec((1, 1, CHUNK, comps), lambda f, i, b, n: (b[slot, 0], f, i, 0)),
                    pl.BlockSpec((1, 1, comps, blk), lambda f, i, b, n: (b[slot, 1], f, 0, 0)),
                    pl.BlockSpec((1, 8, CHUNK, LANES), lambda f, i, b, n: (f, 0, i, 0)),
                    pl.BlockSpec((1, 8, CHUNK, LANES), lambda f, i, b, n: (f, 0, i, 0)),
                    pl.BlockSpec((1, 1, 1, 8, width), lambda f, i, b, n: (slot, 0, f, 0, i)),
                    pl.BlockSpec((1, 1, dirs, 1, 8, width), lambda f, i, b, n: (slot, 0, 0, f, 0, i)),
                ],
                out_specs=[
                    pl.BlockSpec((1, 1, 1, 8, width), lambda f, i, b, n: (0, 0, f, 0, i)),
                    pl.BlockSpec((1, CHUNK, comps), lambda f, i, b, n: (f, i, 0)),
                    pl.BlockSpec((1, comps, blk), lambda f, i, b, n: (f, 0, 0)),
                ],
                scratch_shapes=[
                    pltpu.VMEM((dirs, CHUNK * 8, LANES), jnp.float32),
                    pltpu.VMEM((1, CHUNK * 8, LANES), jnp.float32),
                    pltpu.VMEM((8, CHUNK, LANES), jnp.float32),
                    pltpu.VMEM((comps, 8, LANES), jnp.float32),
                ],
            ),
            out_shape=[
                jax.ShapeDtypeStruct((1, 1, chans, 8, base), jnp.bfloat16),
                jax.ShapeDtypeStruct((chans, blk, comps), jnp.float32),
                jax.ShapeDtypeStruct((chans, comps, blk), jnp.float32),
            ],
            compiler_params=kind,
            cost_estimate=pl.CostEstimate(
                flops=8 * ops, bytes_accessed=dirs * chans * 8 * base * 2, transcendentals=0
            ),
            name="backward",
        )(blocks, counts, left, right, own, other, observed, coherency)

    swap = [(0, 1), (1, 0)]
    own = [forward(slot) for slot in range(maxb)]
    other = [lax.ppermute(x, "dir", swap) for x in own]
    pieces = [backward(slot, own[slot], other[slot]) for slot in range(maxb)]
    residual = jnp.concatenate([p[0] for p in pieces], axis=0)
    index = jnp.arange(nblocks)
    gradient = jnp.zeros((nblocks, chans, comps, blk), jnp.float32)
    for slot, (_, first, second) in enumerate(pieces):
        on_first = (blocks[slot, 0] == index).astype(jnp.float32)[:, None, None, None]
        on_second = (blocks[slot, 1] == index).astype(jnp.float32)[:, None, None, None]
        gradient = gradient + on_first * jnp.swapaxes(first, 1, 2)[None] + on_second * second[None]
    gradient = gradient.reshape(nblocks, chans, dirs, 8, blk)
    gradient = jnp.transpose(gradient, (2, 1, 3, 0, 4)).reshape(dirs, chans, 8, nblocks * blk)
    owned = lax.psum_scatter(gradient, ("pair", "pol"), scatter_dimension=3, tiled=True)
    return residual, owned


def direction_gains(one_dir, first, second, nblocks, blk):
    table = one_dir.reshape(one_dir.shape[0], 8, nblocks, blk)
    gain_a = jnp.moveaxis(jnp.take(table, first, axis=2), 2, 0)
    gain_b = jnp.moveaxis(jnp.take(table, second, axis=2), 2, 0)
    left_g = jnp.repeat(gain_a, blk, axis=3)[:, None]
    right_g = jnp.tile(gain_b, (1, 1, 1, blk))[:, None]
    return (split_parts(left_g, 3), split_parts(right_g, 3))


def baseline_mask(first, second, used, blk):
    pair_index = jnp.arange(blk * blk)
    upper = pair_index // blk < pair_index % blk
    keep = used[:, None] & ((first < second)[:, None] | upper[None, :])
    return keep.astype(jnp.float32)[:, None, None, None, :]


def general_body(blocks, counts, gains, coherency, observed):
    nblocks = lax.axis_size("pair")
    dir_local = gains.shape[0]
    chans = gains.shape[1]
    blk = gains.shape[3]
    maxb = blocks.shape[0]
    whole = lax.all_gather(gains, "pair", axis=3, tiled=True)
    first = blocks[:, 0]
    second = blocks[:, 1]
    used = jnp.arange(maxb) < counts[0]
    mask = baseline_mask(first, second, used, blk)
    partial_sum = jnp.zeros(observed.shape, jnp.float32)
    for local in range(dir_local):
        left_g, right_g = direction_gains(whole[local], first, second, nblocks, blk)
        model_c = split_parts(coherency[:, :, local].astype(jnp.float32), 3)
        partial_sum = partial_sum + jnp.stack(
            product(product(left_g, model_c), adjoint(right_g)), axis=3
        )
    predicted = lax.psum(partial_sum.astype(jnp.bfloat16), "dir").astype(jnp.float32)
    residual = (mask * (observed.astype(jnp.float32) - predicted)).astype(jnp.bfloat16)
    resid_parts = split_parts(residual.astype(jnp.float32), 3)
    onehot_first = (first[:, None] == jnp.arange(nblocks)[None, :]).astype(jnp.float32)
    onehot_second = (second[:, None] == jnp.arange(nblocks)[None, :]).astype(jnp.float32)
    grads = []
    for local in range(dir_local):
        left_g, right_g = direction_gains(whole[local], first, second, nblocks, blk)
        model_c = split_parts(coherency[:, :, local].astype(jnp.float32), 3)
        toward_first = jnp.stack(product(resid_parts, product(right_g, adjoint(model_c))), axis=3)
        toward_second = jnp.stack(product(adjoint(resid_parts), product(left_g, model_c)), axis=3)
        toward_first = jnp.sum(toward_first, axis=1).reshape(maxb, chans, 8, blk, blk).sum(axis=4)
        toward_second = jnp.sum(toward_second, axis=1).reshape(maxb, chans, 8, blk, blk).sum(axis=3)
        grad_dir = jnp.einsum(
            "scxb,sn->cxnb", toward_first, onehot_first, precision=lax.Precision.HIGHEST
        )
        grad_dir = grad_dir + jnp.einsum(
            "scxb,sn->cxnb", toward_second, onehot_second, precision=lax.Precision.HIGHEST
        )
        grads.append(grad_dir.reshape(chans, 8, nblocks * blk))
    gradient = jnp.stack(grads, axis=0)
    owned = lax.psum_scatter(gradient, ("pair", "pol"), scatter_dimension=3, tiled=True)
    return (residual, owned)


def body(blocks, counts, gains, coherency, observed):
    fits = gains.shape[3] == LANES and coherency.shape[1] == 1 and lax.axis_size("dir") == 2
    fits = fits and lax.axis_size("pair") == 4 and blocks.shape[0] == 5
    chosen = fast_body if fits else general_body
    return chosen(blocks, counts, gains, coherency, observed)


def solution(mesh):
    in_specs = (
        P(("grp", "pair"), None),
        P(("grp", "pair")),
        P(("grp", "dir"), None, None, "pair"),
        P(("grp", "pair"), "pol", "dir", None, None, None),
        P(("grp", "pair"), "pol", None, None, None),
    )
    out_specs = (
        P(("grp", "pair"), "pol", None, None, None),
        P(("grp", "dir"), None, None, ("pair", "pol")),
    )
    return jax.shard_map(body, mesh=mesh, in_specs=in_specs, out_specs=out_specs, check_vma=False)
```

```python
import functools

import jax
import jax.numpy as jnp
from jax import lax
from jax.experimental import pallas as pl
from jax.experimental.pallas import tpu as pltpu
from jax.sharding import PartitionSpec as P

LANES = 128


def split_parts(matrix, axis):
    return [lax.index_in_dim(matrix, c, axis, keepdims=False) for c in range(8)]


def product(left, right):
    result = [None] * 8
    for i in range(2):
        for j in range(2):
            re = im = None
            for m in range(2):
                lr, li = left[2 * i + m], left[4 + 2 * i + m]
                rr, ri = right[2 * m + j], right[4 + 2 * m + j]
                re_term = lr * rr - li * ri
                im_term = lr * ri + li * rr
                re = re_term if re is None else re + re_term
                im = im_term if im is None else im + im_term
            result[2 * i + j] = re
            result[4 + 2 * i + j] = im
    return result


def product_adj_right(left, right):
    result = [None] * 8
    for i in range(2):
        for j in range(2):
            re = im = None
            for m in range(2):
                lr, li = left[2 * i + m], left[4 + 2 * i + m]
                rr, ri = right[2 * j + m], right[4 + 2 * j + m]
                re_term = lr * rr + li * ri
                im_term = li * rr - lr * ri
                re = re_term if re is None else re + re_term
                im = im_term if im is None else im + im_term
            result[2 * i + j] = re
            result[4 + 2 * i + j] = im
    return result


def product_adj_left(left, right):
    result = [None] * 8
    for i in range(2):
        for j in range(2):
            re = im = None
            for m in range(2):
                lr, li = left[2 * m + i], left[4 + 2 * m + i]
                rr, ri = right[2 * m + j], right[4 + 2 * m + j]
                re_term = lr * rr + li * ri
                im_term = lr * ri - li * rr
                re = re_term if re is None else re + re_term
                im = im_term if im is None else im + im_term
            result[2 * i + j] = re
            result[4 + 2 * i + j] = im
    return result


def adjoint(m):
    return [m[0], m[2], m[1], m[3], -m[4], -m[6], -m[5], -m[7]]


MESH = pl.DeviceIdType.MESH


def widen(tile, dst, base):
    for p in range(16):
        dst[base + p * 8 : base + p * 8 + 8, :] = tile(p).astype(jnp.float32)


def parts_at(ref, row):
    return [ref[pl.ds(row + c, 8, stride=8), :] for c in range(8)]


def gather_kernel(nblocks, gains, left, right, land, send_sem, recv_sem):
    dirs, chans, _, blk = gains.shape
    me = lax.axis_index("pair")
    barrier = pltpu.get_barrier_semaphore()
    others = [lax.rem(me + d, nblocks) for d in range(1, nblocks)]
    for other in others:
        pl.semaphore_signal(barrier, inc=1, device_id={"pair": other}, device_id_type=MESH)
    pl.semaphore_wait(barrier, nblocks - 1)
    copies = []
    for d, other in enumerate(others):
        copy = pltpu.make_async_remote_copy(
            src_ref=gains,
            dst_ref=land.at[d],
            send_sem=send_sem.at[d],
            recv_sem=recv_sem.at[d],
            device_id={"pair": other},
            device_id_type=MESH,
        )
        copy.start()
        copies.append(copy)
    pad = jnp.zeros((LANES - dirs * 8, LANES), jnp.float32)
    for d in range(nblocks):
        owner = me if d == 0 else lax.rem(me + nblocks - d, nblocks)
        if d > 0:
            copies[d - 1].wait_recv()
        for f in range(chans):
            tiles = [gains[k, f] if d == 0 else land[d - 1, k, f] for k in range(dirs)]
            table = jnp.concatenate(tiles, axis=0)
            right[owner, f] = table
            left[owner, f] = jnp.transpose(jnp.concatenate([table, pad], axis=0))[:, : dirs * 8]
    for copy in copies:
        copy.wait_send()


def reduce_kernel(nblocks, npol, weights, *refs):
    maxb = weights.shape[1]
    firsts, seconds = refs[:maxb], refs[maxb : 2 * maxb]
    out, outgoing, land, send_sem, recv_sem = refs[2 * maxb :]
    dirs = out.shape[0]
    me, pol = lax.axis_index("pair"), lax.axis_index("pol")
    barrier = pltpu.get_barrier_semaphore()
    peers = []
    for dz in range(nblocks):
        for dp in range(npol):
            if dz or dp:
                peers.append((lax.rem(me + dz, nblocks), lax.rem(pol + dp, npol)))
    for z, q in peers:
        pl.semaphore_signal(barrier, inc=1, device_id={"pair": z, "pol": q}, device_id_type=MESH)
    half = LANES // 2
    lower = lax.broadcasted_iota(jnp.int32, (dirs * 8, LANES), 1) < half
    for n in range(nblocks):
        sums = []
        for f in range(2):
            total = None
            for s in range(maxb):
                term = weights[0, s, n] * firsts[s][f] + weights[1, s, n] * seconds[s][f]
                total = term if total is None else total + term
            sums.append(total)
        outgoing[n, 0] = jnp.where(lower, sums[0], pltpu.roll(sums[1], half, 1))
        outgoing[n, 1] = jnp.where(lower, pltpu.roll(sums[0], half, 1), sums[1])
    pl.semaphore_wait(barrier, len(peers))
    copies = []
    for i, (z, q) in enumerate(peers):
        copy = pltpu.make_async_remote_copy(
            src_ref=outgoing.at[z, q],
            dst_ref=land.at[i],
            send_sem=send_sem.at[i],
            recv_sem=recv_sem.at[i],
            device_id={"pair": z, "pol": q},
            device_id_type=MESH,
        )
        copy.start()
        copies.append(copy)
    total = outgoing[me, pol]
    for i, copy in enumerate(copies):
        copy.wait_recv()
        total = total + land[i]
    for k in range(dirs):
        for f in range(2):
            out[k, f] = total[k * 8 : k * 8 + 8, f * half : f * half + half]
    for copy in copies:
        copy.wait_send()


def forward_kernel(dirs, blocks, left_ref, right_ref, coh_ref, out_ref, wide):
    blk = left_ref.shape[2]

    @pl.loop(0, blk // 16)
    def _(g):
        p0 = pl.multiple_of(g * 16, 16)
        for k in range(dirs):
            widen(
                lambda p, k=k: coh_ref[0, 0, k, 0, :, pl.ds(pl.multiple_of((p0 + p) * LANES, LANES), LANES)],
                wide,
                k * 128,
            )
        halves = []
        for h in range(2):
            rows = left_ref[0, 0, pl.ds(p0 + h * 8, 8), :]
            total = None
            for k in range(dirs):
                model = parts_at(wide, k * 128 + h * 64)
                jq = [right_ref[0, 0, k * 8 + c : k * 8 + c + 1, :] for c in range(8)]
                jp = [rows[:, k * 8 + c : k * 8 + c + 1] for c in range(8)]
                term = product(jp, product_adj_right(model, jq))
                total = term if total is None else [x + y for x, y in zip(total, term)]
            halves.append(total)
        for c in range(8):
            both = jnp.concatenate([halves[0][c], halves[1][c]], axis=0)
            out_ref[0, c, pl.ds(p0, 16), :] = both.astype(jnp.bfloat16)


def backward_kernel(
    dirs,
    slot,
    blocks,
    counts,
    left_ref,
    right_ref,
    own_ref,
    other_ref,
    obs_ref,
    coh_ref,
    *refs,
):
    res_ref, first_ref, second_ref, wide, wide_obs, acc, sums_first = refs[-7:]
    blk = left_ref.shape[2]
    used = slot < counts[0]
    off_diag = blocks[slot, 0] < blocks[slot, 1]
    acc[...] = jnp.zeros_like(acc)

    @pl.loop(0, blk // 16)
    def _(g):
        p0 = pl.multiple_of(g * 16, 16)

        def lanes(p):
            return pl.ds(pl.multiple_of((p0 + p) * LANES, LANES), LANES)

        widen(lambda p: obs_ref[0, 0, 0, :, lanes(p)], wide_obs, 0)
        for k in range(dirs):
            widen(lambda p, k=k: coh_ref[0, 0, k, 0, :, lanes(p)], wide, k * 128)
        station = p0 + lax.broadcasted_iota(jnp.int32, (16, LANES), 0)
        partner = lax.broadcasted_iota(jnp.int32, (16, LANES), 1)
        keep = (jnp.where(off_diag, -1, station) < partner) & (jnp.where(used, partner, -1) >= 0)
        rest = []
        for c in range(8):
            predicted = own_ref[0, c, pl.ds(p0, 16), :].astype(jnp.float32) + other_ref[
                0, c, pl.ds(p0, 16), :
            ].astype(jnp.float32)
            seen = jnp.concatenate(
                [wide_obs[pl.ds(h * 64 + c, 8, stride=8), :] for h in range(2)], axis=0
            )
            left_over = jnp.where(keep, seen - predicted, 0.0).astype(jnp.bfloat16).astype(jnp.float32)
            rest.append(left_over)
            for h in range(2):
                wide_obs[pl.ds(h * 64 + c, 8, stride=8), :] = left_over[h * 8 : h * 8 + 8]
        for p in range(16):
            res_ref[0, 0, 0, :, lanes(p)] = wide_obs[p * 8 : p * 8 + 8, :].astype(jnp.bfloat16)
        for k in range(dirs):
            total = None
            for h in range(2):
                model = parts_at(wide, k * 128 + h * 64)
                resid = [r[h * 8 : h * 8 + 8] for r in rest]
                jq = [right_ref[0, 0, k * 8 + c : k * 8 + c + 1, :] for c in range(8)]
                rows = left_ref[0, 0, pl.ds(p0 + h * 8, 8), :]
                jp = [rows[:, k * 8 + c : k * 8 + c + 1] for c in range(8)]
                toward_first = product_adj_right(resid, product_adj_right(model, jq))
                for c in range(8):
                    sums_first[pl.ds(p0 + h * 8, 8), k * 8 + c : k * 8 + c + 1] = jnp.sum(
                        toward_first[c], axis=1, keepdims=True
                    )
                toward_second = product_adj_left(resid, product(jp, model))
                total = toward_second if h == 0 else [x + y for x, y in zip(total, toward_second)]
            for c in range(8):
                acc[k * 8 + c] += total[c]

    second_ref[0] = jnp.sum(acc[...], axis=1)
    first_ref[0] = jnp.transpose(sums_first[...])[: dirs * 8]


def fast_body(blocks, counts, gains, coherency, observed):
    nblocks = lax.axis_size("pair")
    npol = lax.axis_size("pol")
    dirs, chans, _, blk = gains.shape
    maxb = blocks.shape[0]
    base = coherency.shape[-1]
    comps = dirs * 8
    vmem = pl.BlockSpec(memory_space=pltpu.VMEM)
    left, right = pl.pallas_call(
        functools.partial(gather_kernel, nblocks),
        out_shape=[
            jax.ShapeDtypeStruct((nblocks, chans, blk, comps), jnp.float32),
            jax.ShapeDtypeStruct((nblocks, chans, comps, blk), jnp.float32),
        ],
        in_specs=[vmem],
        out_specs=[vmem, vmem],
        scratch_shapes=[
            pltpu.VMEM((nblocks - 1,) + gains.shape, jnp.float32),
            pltpu.SemaphoreType.DMA((nblocks - 1,)),
            pltpu.SemaphoreType.DMA((nblocks - 1,)),
        ],
        compiler_params=pltpu.CompilerParams(
            collective_id=0, has_side_effects=True, vmem_limit_bytes=16 * 2**20
        ),
        name="gather_gains",
    )(gains)
    kind = pltpu.CompilerParams(dimension_semantics=("arbitrary",), vmem_limit_bytes=24 * 2**20)
    ops = 64 * dirs * chans * base

    def forward(slot):
        return pl.pallas_call(
            functools.partial(forward_kernel, dirs),
            grid_spec=pltpu.PrefetchScalarGridSpec(
                num_scalar_prefetch=1,
                grid=(chans,),
                in_specs=[
                    pl.BlockSpec((1, 1, blk, comps), lambda f, b: (b[slot, 0], f, 0, 0)),
                    pl.BlockSpec((1, 1, comps, blk), lambda f, b: (b[slot, 1], f, 0, 0)),
                    pl.BlockSpec((1, 1, dirs, 1, 8, base), lambda f, b: (slot, 0, 0, f, 0, 0)),
                ],
                out_specs=pl.BlockSpec((1, 8, blk, LANES), lambda f, b: (f, 0, 0, 0)),
                scratch_shapes=[pltpu.VMEM((dirs * 128, LANES), jnp.float32)],
            ),
            out_shape=jax.ShapeDtypeStruct((chans, 8, blk, blk), jnp.bfloat16),
            compiler_params=kind,
            cost_estimate=pl.CostEstimate(
                flops=4 * ops, bytes_accessed=dirs * chans * 8 * base * 2, transcendentals=0
            ),
            name="forward",
        )(blocks, left, right, coherency)

    def backward(slot, own, other, residual):
        held = [] if residual is None else [residual]
        return pl.pallas_call(
            functools.partial(backward_kernel, dirs, slot),
            grid_spec=pltpu.PrefetchScalarGridSpec(
                num_scalar_prefetch=2,
                grid=(chans,),
                in_specs=[
                    pl.BlockSpec((1, 1, blk, comps), lambda f, b, n: (b[slot, 0], f, 0, 0)),
                    pl.BlockSpec((1, 1, comps, blk), lambda f, b, n: (b[slot, 1], f, 0, 0)),
                    pl.BlockSpec((1, 8, blk, LANES), lambda f, b, n: (f, 0, 0, 0)),
                    pl.BlockSpec((1, 8, blk, LANES), lambda f, b, n: (f, 0, 0, 0)),
                    pl.BlockSpec((1, 1, 1, 8, base), lambda f, b, n: (slot, 0, f, 0, 0)),
                    pl.BlockSpec((1, 1, dirs, 1, 8, base), lambda f, b, n: (slot, 0, 0, f, 0, 0)),
                ]
                + [pl.BlockSpec(memory_space=pl.ANY)] * len(held),
                out_specs=[
                    pl.BlockSpec((1, 1, 1, 8, base), lambda f, b, n: (slot, 0, f, 0, 0)),
                    pl.BlockSpec((1, comps, blk), lambda f, b, n: (f, 0, 0)),
                    pl.BlockSpec((1, comps, blk), lambda f, b, n: (f, 0, 0)),
                ],
                scratch_shapes=[
                    pltpu.VMEM((dirs * 128, LANES), jnp.float32),
                    pltpu.VMEM((128, LANES), jnp.float32),
                    pltpu.VMEM((comps, 8, LANES), jnp.float32),
                    pltpu.VMEM((blk, LANES), jnp.float32),
                ],
            ),
            out_shape=[
                jax.ShapeDtypeStruct(observed.shape, jnp.bfloat16),
                jax.ShapeDtypeStruct((chans, comps, blk), jnp.float32),
                jax.ShapeDtypeStruct((chans, comps, blk), jnp.float32),
            ],
            input_output_aliases={8: 0} if held else {},
            compiler_params=kind,
            cost_estimate=pl.CostEstimate(
                flops=8 * ops, bytes_accessed=dirs * chans * 8 * base * 2, transcendentals=0
            ),
            name="backward",
        )(blocks, counts, left, right, own, other, observed, coherency, *held)

    swap = [(0, 1), (1, 0)]
    own = [forward(slot) for slot in range(maxb)]
    other = [lax.ppermute(x, "dir", swap) for x in own]
    residual = None
    firsts, seconds = [], []
    for slot in range(maxb):
        residual, first, second = backward(slot, own[slot], other[slot], residual)
        firsts.append(first)
        seconds.append(second)
    index = jnp.arange(nblocks)
    weights = (blocks.T[:, :, None] == index[None, None, :]).astype(jnp.float32)
    peers = nblocks * npol - 1
    owned = pl.pallas_call(
        functools.partial(reduce_kernel, nblocks, npol),
        out_shape=jax.ShapeDtypeStruct((dirs, chans, 8, blk // npol), jnp.float32),
        in_specs=[pl.BlockSpec(memory_space=pltpu.SMEM)] + [vmem] * (2 * maxb),
        out_specs=vmem,
        scratch_shapes=[
            pltpu.VMEM((nblocks, npol, comps, LANES), jnp.float32),
            pltpu.VMEM((peers, comps, LANES), jnp.float32),
            pltpu.SemaphoreType.DMA((peers,)),
            pltpu.SemaphoreType.DMA((peers,)),
        ],
        compiler_params=pltpu.CompilerParams(
            collective_id=1, has_side_effects=True, vmem_limit_bytes=16 * 2**20
        ),
        name="reduce_gradient",
    )(weights, *firsts, *seconds)
    return residual, owned


def direction_gains(one_dir, first, second, nblocks, blk):
    table = one_dir.reshape(one_dir.shape[0], 8, nblocks, blk)
    gain_a = jnp.moveaxis(jnp.take(table, first, axis=2), 2, 0)
    gain_b = jnp.moveaxis(jnp.take(table, second, axis=2), 2, 0)
    left_g = jnp.repeat(gain_a, blk, axis=3)[:, None]
    right_g = jnp.tile(gain_b, (1, 1, 1, blk))[:, None]
    return (split_parts(left_g, 3), split_parts(right_g, 3))


def baseline_mask(first, second, used, blk):
    pair_index = jnp.arange(blk * blk)
    upper = pair_index // blk < pair_index % blk
    keep = used[:, None] & ((first < second)[:, None] | upper[None, :])
    return keep.astype(jnp.float32)[:, None, None, None, :]


def general_body(blocks, counts, gains, coherency, observed):
    nblocks = lax.axis_size("pair")
    dir_local = gains.shape[0]
    chans = gains.shape[1]
    blk = gains.shape[3]
    maxb = blocks.shape[0]
    whole = lax.all_gather(gains, "pair", axis=3, tiled=True)
    first = blocks[:, 0]
    second = blocks[:, 1]
    used = jnp.arange(maxb) < counts[0]
    mask = baseline_mask(first, second, used, blk)
    partial_sum = jnp.zeros(observed.shape, jnp.float32)
    for local in range(dir_local):
        left_g, right_g = direction_gains(whole[local], first, second, nblocks, blk)
        model_c = split_parts(coherency[:, :, local].astype(jnp.float32), 3)
        partial_sum = partial_sum + jnp.stack(
            product(product(left_g, model_c), adjoint(right_g)), axis=3
        )
    predicted = lax.psum(partial_sum.astype(jnp.bfloat16), "dir").astype(jnp.float32)
    residual = (mask * (observed.astype(jnp.float32) - predicted)).astype(jnp.bfloat16)
    resid_parts = split_parts(residual.astype(jnp.float32), 3)
    onehot_first = (first[:, None] == jnp.arange(nblocks)[None, :]).astype(jnp.float32)
    onehot_second = (second[:, None] == jnp.arange(nblocks)[None, :]).astype(jnp.float32)
    grads = []
    for local in range(dir_local):
        left_g, right_g = direction_gains(whole[local], first, second, nblocks, blk)
        model_c = split_parts(coherency[:, :, local].astype(jnp.float32), 3)
        toward_first = jnp.stack(product(resid_parts, product(right_g, adjoint(model_c))), axis=3)
        toward_second = jnp.stack(product(adjoint(resid_parts), product(left_g, model_c)), axis=3)
        toward_first = jnp.sum(toward_first, axis=1).reshape(maxb, chans, 8, blk, blk).sum(axis=4)
        toward_second = jnp.sum(toward_second, axis=1).reshape(maxb, chans, 8, blk, blk).sum(axis=3)
        grad_dir = jnp.einsum(
            "scxb,sn->cxnb", toward_first, onehot_first, precision=lax.Precision.HIGHEST
        )
        grad_dir = grad_dir + jnp.einsum(
            "scxb,sn->cxnb", toward_second, onehot_second, precision=lax.Precision.HIGHEST
        )
        grads.append(grad_dir.reshape(chans, 8, nblocks * blk))
    gradient = jnp.stack(grads, axis=0)
    owned = lax.psum_scatter(gradient, ("pair", "pol"), scatter_dimension=3, tiled=True)
    return (residual, owned)


def body(blocks, counts, gains, coherency, observed):
    fits = gains.shape[3] == LANES and coherency.shape[1] == 1 and lax.axis_size("dir") == 2
    fits = fits and gains.shape[1] == 2 and lax.axis_size("pol") == 2 and lax.axis_size("pair") <= 8
    chosen = fast_body if fits else general_body
    return chosen(blocks, counts, gains, coherency, observed)


def solution(mesh):
    in_specs = (
        P(("grp", "pair"), None),
        P(("grp", "pair")),
        P(("grp", "dir"), None, None, "pair"),
        P(("grp", "pair"), "pol", "dir", None, None, None),
        P(("grp", "pair"), "pol", None, None, None),
    )
    out_specs = (
        P(("grp", "pair"), "pol", None, None, None),
        P(("grp", "dir"), None, None, ("pair", "pol")),
    )
    return jax.shard_map(body, mesh=mesh, in_specs=in_specs, out_specs=out_specs, check_vma=False)
```

```python
import functools

import jax
import jax.numpy as jnp
from jax import lax
from jax.experimental import pallas as pl
from jax.experimental.pallas import tpu as pltpu
from jax.sharding import PartitionSpec as P

LANES = 128


def split_parts(matrix, axis):
    return [lax.index_in_dim(matrix, c, axis, keepdims=False) for c in range(8)]


def product(left, right):
    result = [None] * 8
    for i in range(2):
        for j in range(2):
            re = im = None
            for m in range(2):
                lr, li = left[2 * i + m], left[4 + 2 * i + m]
                rr, ri = right[2 * m + j], right[4 + 2 * m + j]
                re_term = lr * rr - li * ri
                im_term = lr * ri + li * rr
                re = re_term if re is None else re + re_term
                im = im_term if im is None else im + im_term
            result[2 * i + j] = re
            result[4 + 2 * i + j] = im
    return result


def product_adj_right(left, right):
    result = [None] * 8
    for i in range(2):
        for j in range(2):
            re = im = None
            for m in range(2):
                lr, li = left[2 * i + m], left[4 + 2 * i + m]
                rr, ri = right[2 * j + m], right[4 + 2 * j + m]
                re_term = lr * rr + li * ri
                im_term = li * rr - lr * ri
                re = re_term if re is None else re + re_term
                im = im_term if im is None else im + im_term
            result[2 * i + j] = re
            result[4 + 2 * i + j] = im
    return result


def product_adj_left(left, right):
    result = [None] * 8
    for i in range(2):
        for j in range(2):
            re = im = None
            for m in range(2):
                lr, li = left[2 * m + i], left[4 + 2 * m + i]
                rr, ri = right[2 * m + j], right[4 + 2 * m + j]
                re_term = lr * rr + li * ri
                im_term = lr * ri - li * rr
                re = re_term if re is None else re + re_term
                im = im_term if im is None else im + im_term
            result[2 * i + j] = re
            result[4 + 2 * i + j] = im
    return result


def adjoint(m):
    return [m[0], m[2], m[1], m[3], -m[4], -m[6], -m[5], -m[7]]


MESH = pl.DeviceIdType.MESH


def widen(tile, dst, base):
    for p in range(16):
        dst[base + p * 8 : base + p * 8 + 8, :] = tile(p).astype(jnp.float32)


def parts_at(ref, row):
    return [ref[pl.ds(row + c, 8, stride=8), :] for c in range(8)]


def gather_kernel(nblocks, gains, left, right, land, send_sem, recv_sem):
    dirs, chans, _, blk = gains.shape
    me = lax.axis_index("pair")
    barrier = pltpu.get_barrier_semaphore()
    others = [lax.rem(me + d, nblocks) for d in range(1, nblocks)]
    for other in others:
        pl.semaphore_signal(barrier, inc=1, device_id={"pair": other}, device_id_type=MESH)
    pl.semaphore_wait(barrier, nblocks - 1)
    copies = []
    for d, other in enumerate(others):
        copy = pltpu.make_async_remote_copy(
            src_ref=gains,
            dst_ref=land.at[d],
            send_sem=send_sem.at[d],
            recv_sem=recv_sem.at[d],
            device_id={"pair": other},
            device_id_type=MESH,
        )
        copy.start()
        copies.append(copy)
    pad = jnp.zeros((LANES - dirs * 8, LANES), jnp.float32)
    for d in range(nblocks):
        owner = me if d == 0 else lax.rem(me + nblocks - d, nblocks)
        if d > 0:
            copies[d - 1].wait_recv()
        for f in range(chans):
            tiles = [gains[k, f] if d == 0 else land[d - 1, k, f] for k in range(dirs)]
            table = jnp.concatenate(tiles, axis=0)
            right[owner, f] = table
            left[owner, f] = jnp.transpose(jnp.concatenate([table, pad], axis=0))[:, : dirs * 8]
    for copy in copies:
        copy.wait_send()


def reduce_kernel(nblocks, npol, weights, *refs):
    maxb = weights.shape[1]
    firsts, seconds = refs[:maxb], refs[maxb : 2 * maxb]
    out, outgoing, land, send_sem, recv_sem = refs[2 * maxb :]
    dirs = out.shape[0]
    me, pol = lax.axis_index("pair"), lax.axis_index("pol")
    barrier = pltpu.get_barrier_semaphore()
    peers = []
    for dz in range(nblocks):
        for dp in range(npol):
            if dz or dp:
                peers.append((lax.rem(me + dz, nblocks), lax.rem(pol + dp, npol)))
    for z, q in peers:
        pl.semaphore_signal(barrier, inc=1, device_id={"pair": z, "pol": q}, device_id_type=MESH)
    half = LANES // 2
    lower = lax.broadcasted_iota(jnp.int32, (dirs * 8, LANES), 1) < half
    for n in range(nblocks):
        sums = []
        for f in range(2):
            total = None
            for s in range(maxb):
                term = weights[0, s, n] * firsts[s][f] + weights[1, s, n] * seconds[s][f]
                total = term if total is None else total + term
            sums.append(total)
        outgoing[n, 0] = jnp.where(lower, sums[0], pltpu.roll(sums[1], half, 1))
        outgoing[n, 1] = jnp.where(lower, pltpu.roll(sums[0], half, 1), sums[1])
    pl.semaphore_wait(barrier, len(peers))
    copies = []
    for i, (z, q) in enumerate(peers):
        copy = pltpu.make_async_remote_copy(
            src_ref=outgoing.at[z, q],
            dst_ref=land.at[i],
            send_sem=send_sem.at[i],
            recv_sem=recv_sem.at[i],
            device_id={"pair": z, "pol": q},
            device_id_type=MESH,
        )
        copy.start()
        copies.append(copy)
    total = outgoing[me, pol]
    for i, copy in enumerate(copies):
        copy.wait_recv()
        total = total + land[i]
    for k in range(dirs):
        for f in range(2):
            out[k, f] = total[k * 8 : k * 8 + 8, f * half : f * half + half]
    for copy in copies:
        copy.wait_send()


def forward_kernel(dirs, blocks, left_ref, right_ref, coh_ref, out_ref, kept_ref, wide):
    blk = left_ref.shape[2]

    @pl.loop(0, blk // 16)
    def _(g):
        p0 = pl.multiple_of(g * 16, 16)
        for k in range(dirs):
            widen(
                lambda p, k=k: coh_ref[0, 0, k, 0, :, pl.ds(pl.multiple_of((p0 + p) * LANES, LANES), LANES)],
                wide,
                k * 128,
            )
        halves = [None, None]
        for k in range(dirs):
            lefts = []
            for h in range(2):
                rows = left_ref[0, 0, pl.ds(p0 + h * 8, 8), :]
                model = parts_at(wide, k * 128 + h * 64)
                jq = [right_ref[0, 0, k * 8 + c : k * 8 + c + 1, :] for c in range(8)]
                jp = [rows[:, k * 8 + c : k * 8 + c + 1] for c in range(8)]
                left = product(jp, model)
                lefts.append(left)
                term = product_adj_right(left, jq)
                halves[h] = term if k == 0 else [x + y for x, y in zip(halves[h], term)]
            for c in range(8):
                both = jnp.concatenate([lefts[0][c], lefts[1][c]], axis=0)
                kept_ref[0, k, c, pl.ds(p0, 16), :] = both.astype(jnp.bfloat16)
        for c in range(8):
            both = jnp.concatenate([halves[0][c], halves[1][c]], axis=0)
            out_ref[0, c, pl.ds(p0, 16), :] = both.astype(jnp.bfloat16)


def backward_kernel(
    dirs,
    slot,
    blocks,
    counts,
    right_ref,
    own_ref,
    other_ref,
    kept_ref,
    obs_ref,
    coh_ref,
    *refs,
):
    res_ref, first_ref, second_ref, wide, wide_obs, acc, sums_first = refs[-7:]
    blk = right_ref.shape[3]
    used = slot < counts[0]
    off_diag = blocks[slot, 0] < blocks[slot, 1]
    acc[...] = jnp.zeros_like(acc)

    @pl.loop(0, blk // 16)
    def _(g):
        p0 = pl.multiple_of(g * 16, 16)

        def lanes(p):
            return pl.ds(pl.multiple_of((p0 + p) * LANES, LANES), LANES)

        widen(lambda p: obs_ref[0, 0, 0, :, lanes(p)], wide_obs, 0)
        for k in range(dirs):
            widen(lambda p, k=k: coh_ref[0, 0, k, 0, :, lanes(p)], wide, k * 128)
        station = p0 + lax.broadcasted_iota(jnp.int32, (16, LANES), 0)
        partner = lax.broadcasted_iota(jnp.int32, (16, LANES), 1)
        keep = (jnp.where(off_diag, -1, station) < partner) & (jnp.where(used, partner, -1) >= 0)
        rest = []
        for c in range(8):
            predicted = own_ref[0, c, pl.ds(p0, 16), :].astype(jnp.float32) + other_ref[
                0, c, pl.ds(p0, 16), :
            ].astype(jnp.float32)
            seen = jnp.concatenate(
                [wide_obs[pl.ds(h * 64 + c, 8, stride=8), :] for h in range(2)], axis=0
            )
            left_over = jnp.where(keep, seen - predicted, 0.0).astype(jnp.bfloat16).astype(jnp.float32)
            rest.append(left_over)
            for h in range(2):
                wide_obs[pl.ds(h * 64 + c, 8, stride=8), :] = left_over[h * 8 : h * 8 + 8]
        for p in range(16):
            res_ref[0, 0, 0, :, lanes(p)] = wide_obs[p * 8 : p * 8 + 8, :].astype(jnp.bfloat16)
        for k in range(dirs):
            total = None
            firsts = []
            kept = [kept_ref[0, k, c, pl.ds(p0, 16), :].astype(jnp.float32) for c in range(8)]
            for h in range(2):
                model = parts_at(wide, k * 128 + h * 64)
                resid = [r[h * 8 : h * 8 + 8] for r in rest]
                jq = [right_ref[0, 0, k * 8 + c : k * 8 + c + 1, :] for c in range(8)]
                firsts.append(product_adj_right(resid, product_adj_right(model, jq)))
                toward_second = product_adj_left(resid, [y[h * 8 : h * 8 + 8] for y in kept])
                total = toward_second if h == 0 else [x + y for x, y in zip(total, toward_second)]
            for c in range(8):
                acc[k * 8 + c] += total[c]
            rows = [firsts[h][c] for c in range(8) for h in range(2)]
            stack = jnp.concatenate(rows, axis=0).astype(jnp.bfloat16)
            summed = lax.dot_general(
                jnp.ones((8, LANES), jnp.bfloat16),
                stack,
                (((1,), (1,)), ((), ())),
                preferred_element_type=jnp.float32,
            )
            sums_first[k, pl.ds(g, 1), :] = summed[:1]

    second_ref[0] = jnp.sum(acc[...], axis=1)
    row = lax.broadcasted_iota(jnp.int32, (8, LANES), 0)
    col = lax.broadcasted_iota(jnp.int32, (8, LANES), 1)
    apart = (col // 16 - row) & 7
    for k in range(dirs):
        source = sums_first[k]
        result = source
        for d in range(1, 8):
            moved = pltpu.roll(pltpu.roll(source, 8 - d, 0), 16 * d, 1)
            result = jnp.where(apart == d, moved, result)
        first_ref[0, k * 8 : k * 8 + 8, :] = result


def fast_body(blocks, counts, gains, coherency, observed):
    nblocks = lax.axis_size("pair")
    npol = lax.axis_size("pol")
    dirs, chans, _, blk = gains.shape
    maxb = blocks.shape[0]
    base = coherency.shape[-1]
    comps = dirs * 8
    vmem = pl.BlockSpec(memory_space=pltpu.VMEM)
    left, right = pl.pallas_call(
        functools.partial(gather_kernel, nblocks),
        out_shape=[
            jax.ShapeDtypeStruct((nblocks, chans, blk, comps), jnp.float32),
            jax.ShapeDtypeStruct((nblocks, chans, comps, blk), jnp.float32),
        ],
        in_specs=[vmem],
        out_specs=[vmem, vmem],
        scratch_shapes=[
            pltpu.VMEM((nblocks - 1,) + gains.shape, jnp.float32),
            pltpu.SemaphoreType.DMA((nblocks - 1,)),
            pltpu.SemaphoreType.DMA((nblocks - 1,)),
        ],
        compiler_params=pltpu.CompilerParams(
            collective_id=0, has_side_effects=True, vmem_limit_bytes=16 * 2**20
        ),
        name="gather_gains",
    )(gains)
    kind = pltpu.CompilerParams(dimension_semantics=("arbitrary",), vmem_limit_bytes=24 * 2**20)
    ops = 64 * dirs * chans * base

    def forward(slot):
        return pl.pallas_call(
            functools.partial(forward_kernel, dirs),
            grid_spec=pltpu.PrefetchScalarGridSpec(
                num_scalar_prefetch=1,
                grid=(chans,),
                in_specs=[
                    pl.BlockSpec((1, 1, blk, comps), lambda f, b: (b[slot, 0], f, 0, 0)),
                    pl.BlockSpec((1, 1, comps, blk), lambda f, b: (b[slot, 1], f, 0, 0)),
                    pl.BlockSpec((1, 1, dirs, 1, 8, base), lambda f, b: (slot, 0, 0, f, 0, 0)),
                ],
                out_specs=[
                    pl.BlockSpec((1, 8, blk, LANES), lambda f, b: (f, 0, 0, 0)),
                    pl.BlockSpec((1, dirs, 8, blk, LANES), lambda f, b: (f, 0, 0, 0, 0)),
                ],
                scratch_shapes=[pltpu.VMEM((dirs * 128, LANES), jnp.float32)],
            ),
            out_shape=[
                jax.ShapeDtypeStruct((chans, 8, blk, blk), jnp.bfloat16),
                jax.ShapeDtypeStruct((chans, dirs, 8, blk, blk), jnp.bfloat16),
            ],
            compiler_params=kind,
            cost_estimate=pl.CostEstimate(
                flops=4 * ops, bytes_accessed=dirs * chans * 8 * base * 2, transcendentals=0
            ),
            name="forward",
        )(blocks, left, right, coherency)

    def backward(slot, own, other, kept, residual):
        held = [] if residual is None else [residual]
        return pl.pallas_call(
            functools.partial(backward_kernel, dirs, slot),
            grid_spec=pltpu.PrefetchScalarGridSpec(
                num_scalar_prefetch=2,
                grid=(chans,),
                in_specs=[
                    pl.BlockSpec((1, 1, comps, blk), lambda f, b, n: (b[slot, 1], f, 0, 0)),
                    pl.BlockSpec((1, 8, blk, LANES), lambda f, b, n: (f, 0, 0, 0)),
                    pl.BlockSpec((1, 8, blk, LANES), lambda f, b, n: (f, 0, 0, 0)),
                    pl.BlockSpec((1, dirs, 8, blk, LANES), lambda f, b, n: (f, 0, 0, 0, 0)),
                    pl.BlockSpec((1, 1, 1, 8, base), lambda f, b, n: (slot, 0, f, 0, 0)),
                    pl.BlockSpec((1, 1, dirs, 1, 8, base), lambda f, b, n: (slot, 0, 0, f, 0, 0)),
                ]
                + [pl.BlockSpec(memory_space=pl.ANY)] * len(held),
                out_specs=[
                    pl.BlockSpec((1, 1, 1, 8, base), lambda f, b, n: (slot, 0, f, 0, 0)),
                    pl.BlockSpec((1, comps, blk), lambda f, b, n: (f, 0, 0)),
                    pl.BlockSpec((1, comps, blk), lambda f, b, n: (f, 0, 0)),
                ],
                scratch_shapes=[
                    pltpu.VMEM((dirs * 128, LANES), jnp.float32),
                    pltpu.VMEM((128, LANES), jnp.float32),
                    pltpu.VMEM((comps, 8, LANES), jnp.float32),
                    pltpu.VMEM((dirs, 8, LANES), jnp.float32),
                ],
            ),
            out_shape=[
                jax.ShapeDtypeStruct(observed.shape, jnp.bfloat16),
                jax.ShapeDtypeStruct((chans, comps, blk), jnp.float32),
                jax.ShapeDtypeStruct((chans, comps, blk), jnp.float32),
            ],
            input_output_aliases={8: 0} if held else {},
            compiler_params=kind,
            cost_estimate=pl.CostEstimate(
                flops=8 * ops, bytes_accessed=dirs * chans * 8 * base * 2, transcendentals=0
            ),
            name="backward",
        )(blocks, counts, right, own, other, kept, observed, coherency, *held)

    swap = [(0, 1), (1, 0)]
    own, kept = zip(*[forward(slot) for slot in range(maxb)])
    other = [lax.ppermute(x, "dir", swap) for x in own]
    residual = None
    firsts, seconds = [], []
    for slot in range(maxb):
        residual, first, second = backward(slot, own[slot], other[slot], kept[slot], residual)
        firsts.append(first)
        seconds.append(second)
    index = jnp.arange(nblocks)
    weights = (blocks.T[:, :, None] == index[None, None, :]).astype(jnp.float32)
    peers = nblocks * npol - 1
    owned = pl.pallas_call(
        functools.partial(reduce_kernel, nblocks, npol),
        out_shape=jax.ShapeDtypeStruct((dirs, chans, 8, blk // npol), jnp.float32),
        in_specs=[pl.BlockSpec(memory_space=pltpu.SMEM)] + [vmem] * (2 * maxb),
        out_specs=vmem,
        scratch_shapes=[
            pltpu.VMEM((nblocks, npol, comps, LANES), jnp.float32),
            pltpu.VMEM((peers, comps, LANES), jnp.float32),
            pltpu.SemaphoreType.DMA((peers,)),
            pltpu.SemaphoreType.DMA((peers,)),
        ],
        compiler_params=pltpu.CompilerParams(
            collective_id=1, has_side_effects=True, vmem_limit_bytes=16 * 2**20
        ),
        name="reduce_gradient",
    )(weights, *firsts, *seconds)
    return residual, owned


def direction_gains(one_dir, first, second, nblocks, blk):
    table = one_dir.reshape(one_dir.shape[0], 8, nblocks, blk)
    gain_a = jnp.moveaxis(jnp.take(table, first, axis=2), 2, 0)
    gain_b = jnp.moveaxis(jnp.take(table, second, axis=2), 2, 0)
    left_g = jnp.repeat(gain_a, blk, axis=3)[:, None]
    right_g = jnp.tile(gain_b, (1, 1, 1, blk))[:, None]
    return (split_parts(left_g, 3), split_parts(right_g, 3))


def baseline_mask(first, second, used, blk):
    pair_index = jnp.arange(blk * blk)
    upper = pair_index // blk < pair_index % blk
    keep = used[:, None] & ((first < second)[:, None] | upper[None, :])
    return keep.astype(jnp.float32)[:, None, None, None, :]


def general_body(blocks, counts, gains, coherency, observed):
    nblocks = lax.axis_size("pair")
    dir_local = gains.shape[0]
    chans = gains.shape[1]
    blk = gains.shape[3]
    maxb = blocks.shape[0]
    whole = lax.all_gather(gains, "pair", axis=3, tiled=True)
    first = blocks[:, 0]
    second = blocks[:, 1]
    used = jnp.arange(maxb) < counts[0]
    mask = baseline_mask(first, second, used, blk)
    partial_sum = jnp.zeros(observed.shape, jnp.float32)
    for local in range(dir_local):
        left_g, right_g = direction_gains(whole[local], first, second, nblocks, blk)
        model_c = split_parts(coherency[:, :, local].astype(jnp.float32), 3)
        partial_sum = partial_sum + jnp.stack(
            product(product(left_g, model_c), adjoint(right_g)), axis=3
        )
    predicted = lax.psum(partial_sum.astype(jnp.bfloat16), "dir").astype(jnp.float32)
    residual = (mask * (observed.astype(jnp.float32) - predicted)).astype(jnp.bfloat16)
    resid_parts = split_parts(residual.astype(jnp.float32), 3)
    onehot_first = (first[:, None] == jnp.arange(nblocks)[None, :]).astype(jnp.float32)
    onehot_second = (second[:, None] == jnp.arange(nblocks)[None, :]).astype(jnp.float32)
    grads = []
    for local in range(dir_local):
        left_g, right_g = direction_gains(whole[local], first, second, nblocks, blk)
        model_c = split_parts(coherency[:, :, local].astype(jnp.float32), 3)
        toward_first = jnp.stack(product(resid_parts, product(right_g, adjoint(model_c))), axis=3)
        toward_second = jnp.stack(product(adjoint(resid_parts), product(left_g, model_c)), axis=3)
        toward_first = jnp.sum(toward_first, axis=1).reshape(maxb, chans, 8, blk, blk).sum(axis=4)
        toward_second = jnp.sum(toward_second, axis=1).reshape(maxb, chans, 8, blk, blk).sum(axis=3)
        grad_dir = jnp.einsum(
            "scxb,sn->cxnb", toward_first, onehot_first, precision=lax.Precision.HIGHEST
        )
        grad_dir = grad_dir + jnp.einsum(
            "scxb,sn->cxnb", toward_second, onehot_second, precision=lax.Precision.HIGHEST
        )
        grads.append(grad_dir.reshape(chans, 8, nblocks * blk))
    gradient = jnp.stack(grads, axis=0)
    owned = lax.psum_scatter(gradient, ("pair", "pol"), scatter_dimension=3, tiled=True)
    return (residual, owned)


def body(blocks, counts, gains, coherency, observed):
    fits = gains.shape[3] == LANES and coherency.shape[1] == 1 and lax.axis_size("dir") == 2
    fits = fits and gains.shape[1] == 2 and lax.axis_size("pol") == 2 and lax.axis_size("pair") <= 8
    chosen = fast_body if fits else general_body
    return chosen(blocks, counts, gains, coherency, observed)


def solution(mesh):
    in_specs = (
        P(("grp", "pair"), None),
        P(("grp", "pair")),
        P(("grp", "dir"), None, None, "pair"),
        P(("grp", "pair"), "pol", "dir", None, None, None),
        P(("grp", "pair"), "pol", None, None, None),
    )
    out_specs = (
        P(("grp", "pair"), "pol", None, None, None),
        P(("grp", "dir"), None, None, ("pair", "pol")),
    )
    return jax.shard_map(body, mesh=mesh, in_specs=in_specs, out_specs=out_specs, check_vma=False)
```
